256 devices in a mesh: fsdp: 16 (over y_lo, z), ctx: 16 (over x, y_hi, core).
Axes of the slice: x: 4, y: 4 (y_hi: 2, y_lo: 2; y = y_hi * 2 + y_lo), z: 8, core: 2. Of those that a mesh axis runs over, the one named last changes fastest.
Arguments:
- query_rows: bfloat16 [16, 2048, 2560], P('fsdp', 'ctx'), may hold values from -6 to 6
- key_rows: bfloat16 [16, 2048, 2560], P('fsdp', 'ctx'), may hold values from -6.6 to 6.6
- value_rows: bfloat16 [16, 2048, 2560], P('fsdp', 'ctx'), may hold values from -6 to 6
- query_tangent: bfloat16 [16, 2048, 2560], P('fsdp', 'ctx'), may hold values from -6 to 6
- key_tangent: bfloat16 [16, 2048, 2560], P('fsdp', 'ctx'), may hold values from -6 to 6
- value_tangent: bfloat16 [16, 2048, 2560], P('fsdp', 'ctx'), may hold values from -6 to 6
- cotangent: bfloat16 [16, 2048, 2560], P('fsdp', 'ctx'), may hold values from -6 to 6
- out_weight: bfloat16 [2560, 2560], P('fsdp'), may hold values from -0.125 to 0.125
Outputs:
- tangent_out: bfloat16 [16, 2048, 2560], P('fsdp', 'ctx')
- query_grad: bfloat16 [16, 2048, 2560], P('fsdp', 'ctx')
- key_grad: bfloat16 [16, 2048, 2560], P('fsdp', 'ctx')
- value_grad: bfloat16 [16, 2048, 2560], P('fsdp', 'ctx')
The draws below stay inside these ranges and needn't reach their ends.
All inputs are finite; a program needn't handle non-finite values.
Results may differ from the reference program's by a relative error of at most 0.0163.
Values may be sent and summed in bfloat16 or wider, within the bound.
No kernel may reach another device: no remote copies, remote signals or barrier semaphores. Data moves between devices by JAX's collectives and lax.ppermute only.
A program may use at most 128 MiB of HBM per device.

```python
import jax
import jax.numpy as jnp
from jax import lax

HEADS = 20
HEAD_DIM = 128
OUT_WIDTH = 2560
TOK_DEV = 128
ATT = 2560
LENGTH = 2048
VIDEOS = 16
N_CTX = 16


def base_rows(key):
    return jnp.clip(jax.random.normal(jax.random.fold_in(key, 13), (VIDEOS, LENGTH, ATT), jnp.float32), -6.0, 6.0)


def draw_query_rows(key, part):
    key = jax.random.fold_in(key, 3)
    rows = base_rows(key)
    return rows.astype(jnp.bfloat16)


def draw_key_rows(key, part):
    key = jax.random.fold_in(key, 5)
    rows = base_rows(key)
    return rows.astype(jnp.bfloat16)


def levels(rng, dims, cuts, low, high):
    loudness = 1.0
    for position, shards_of in cuts:
        steps = jax.random.uniform(jax.random.fold_in(jax.random.fold_in(rng, 6), position), (shards_of,), jnp.float32, low / len(cuts), high / len(cuts))
        loudness = loudness * jnp.repeat(jnp.exp(steps), dims[position] // shards_of).reshape((-1,) + (1,) * (len(dims) - 1 - position))
    return loudness


def noise(rng, extent, width, bound, split=(), held_as=jnp.bfloat16):
    level = levels(rng, extent, split, -0.22, 0.18) if split else 1.0
    drawn = jax.random.normal(rng, extent, jnp.float32) * width * level
    return jnp.minimum(jnp.maximum(drawn, -bound), bound).astype(held_as)


def setup_inputs(seed: int = 0) -> dict:
    seeds = jax.random.split(jax.random.key(seed), 9)
    return {
        "query_rows": draw_query_rows(jax.random.fold_in(seeds[8], 71), 0),
        "key_rows": draw_key_rows(jax.random.fold_in(seeds[8], 71), 0),
        "value_rows": noise(seeds[2], (VIDEOS, LENGTH, ATT), 1.0, 6.0, ((0, 16), (1, 16))),
        "query_tangent": noise(seeds[3], (VIDEOS, LENGTH, ATT), 1.0, 6.0, ((0, 16), (1, 16))),
        "key_tangent": noise(seeds[4], (VIDEOS, LENGTH, ATT), 1.0, 6.0, ((0, 16), (1, 16))),
        "value_tangent": noise(seeds[5], (VIDEOS, LENGTH, ATT), 1.0, 6.0, ((0, 16), (1, 16))),
        "cotangent": noise(seeds[6], (VIDEOS, LENGTH, OUT_WIDTH), 1.0, 6.0, ((0, 16), (1, 16))),
        "out_weight": noise(seeds[7], (ATT, OUT_WIDTH), ATT ** -0.5, 0.125, ((0, 16),)),
    }


def heads_view(block):
    return block.astype(jnp.float32).reshape(block.shape[0], HEADS, HEAD_DIM)


def attend(query_block, key_window, value_window, tq_block, tk_window, tv_window, grad_block):
    factor = HEAD_DIM ** -0.5
    query_h = heads_view(query_block)
    key_h = heads_view(key_window)
    value_h = heads_view(value_window)
    tq_h = heads_view(tq_block)
    tk_h = heads_view(tk_window)
    tv_h = heads_view(tv_window)
    grad_h = heads_view(grad_block)
    scores = jnp.einsum('ihd,jhd->hij', query_h, key_h) * factor
    top_score = jnp.max(scores, axis=-1, keepdims=True)
    expos = jnp.exp(scores - top_score)
    weights = expos / jnp.sum(expos, axis=-1, keepdims=True)
    weights_b = weights.astype(jnp.bfloat16).astype(jnp.float32)
    attn = jnp.einsum('hij,jhd->ihd', weights_b, value_h)
    tan_scores = (jnp.einsum('ihd,jhd->hij', tq_h, key_h) + jnp.einsum('ihd,jhd->hij', query_h, tk_h)) * factor
    tan_prob = weights * (tan_scores - jnp.sum(weights * tan_scores, axis=-1, keepdims=True))
    tan_prob_b = tan_prob.astype(jnp.bfloat16).astype(jnp.float32)
    tan_attn = jnp.einsum('hij,jhd->ihd', weights_b, tv_h) + jnp.einsum('hij,jhd->ihd', tan_prob_b, value_h)
    tan_attn = tan_attn.reshape(query_block.shape[0], -1).astype(jnp.bfloat16)
    grad_prob = jnp.einsum('ihd,jhd->hij', grad_h, value_h)
    delta = jnp.einsum('ihd,ihd->hi', grad_h, attn)[:, :, None]
    grad_scores = (weights * (grad_prob - delta) * factor).astype(jnp.bfloat16).astype(jnp.float32)
    query_grad = jnp.einsum('hij,jhd->ihd', grad_scores, key_h).reshape(query_block.shape[0], -1).astype(jnp.bfloat16)
    key_terms = jnp.einsum('hij,ihd->jhd', grad_scores, query_h).reshape(key_window.shape[0], -1)
    value_terms = jnp.einsum('hij,ihd->jhd', weights_b, grad_h).reshape(key_window.shape[0], -1)
    return tan_attn, query_grad, key_terms, value_terms


def one_video(arrays, out_weight):
    query_rows, key_rows, value_rows, query_tangent, key_tangent, value_tangent, cotangent = arrays
    grad_attn = jnp.dot(cotangent, out_weight.T, preferred_element_type=jnp.float32).astype(jnp.bfloat16)

    def blocked(x):
        return x.reshape(N_CTX, TOK_DEV, x.shape[-1])

    qb, kb, vb = blocked(query_rows), blocked(key_rows), blocked(value_rows)
    tqb, tkb, tvb = blocked(query_tangent), blocked(key_tangent), blocked(value_tangent)
    gb = blocked(grad_attn)

    def window(stack, index):
        return jnp.concatenate([stack[(index - 2) % N_CTX], stack[(index - 1) % N_CTX], stack[index]], axis=0)

    def per_block(index):
        return attend(qb[index], window(kb, index), window(vb, index), tqb[index], window(tkb, index), window(tvb, index), gb[index])

    tan_attn, query_grad, key_terms, value_terms = lax.map(per_block, jnp.arange(N_CTX, dtype=jnp.int32))

    def combine(terms):
        parts = terms.reshape(N_CTX, 3, TOK_DEV, ATT)
        total = parts[:, 2] + jnp.roll(parts[:, 1], -1, axis=0) + jnp.roll(parts[:, 0], -2, axis=0)
        return total.reshape(LENGTH, ATT).astype(jnp.bfloat16)

    tangent_out = jnp.dot(tan_attn.reshape(LENGTH, ATT), out_weight, preferred_element_type=jnp.float32).astype(jnp.bfloat16)
    return tangent_out, query_grad.reshape(LENGTH, ATT), combine(key_terms), combine(value_terms)


def reference(query_rows, key_rows, value_rows, query_tangent, key_tangent, value_tangent, cotangent, out_weight):
    return lax.map(lambda arrays: one_video(arrays, out_weight), (query_rows, key_rows, value_rows, query_tangent, key_tangent, value_tangent, cotangent))
```

```python
import functools

import jax
import jax.numpy as jnp
from jax import lax
from jax.experimental import pallas as pl
from jax.experimental.pallas import tpu as pltpu
from jax.sharding import Mesh
from jax.sharding import PartitionSpec as P

HEADS = 20
HEAD_DIM = 128
ROWS = 128
WIDTH = HEADS * HEAD_DIM
HALF = WIDTH // 2
HALF_HEADS = HEADS // 2
FACTOR = HEAD_DIM ** (-0.5)

AXES = ("yl", "z", "x", "yh", "c")
SIZES = (2, 8, 4, 2, 2)

F32 = jnp.float32
BF16 = jnp.bfloat16
VMEM_LIMIT = 48 * 1024 * 1024


def permute(block, move):
    route = []
    for index in range(256):
        rest, place = index, []
        for size in reversed(SIZES):
            place.append(rest % size)
            rest //= size
        goal = 0
        for coordinate, size in zip(move(*reversed(place)), SIZES):
            goal = goal * size + coordinate
        route.append((index, goal))
    return lax.ppermute(block, AXES, route)


def to_chip(step, cross=False):
    def move(yl, z, x, yh, c):
        chip = (x * 2 + yh + step) % 8
        return yl, z, chip // 2, chip % 2, (1 - c if cross else c)

    return move


def to_sibling(yl, z, x, yh, c):
    return yl, z, x, yh, 1 - c


def swap_low_and_core(yl, z, x, yh, c):
    return c, z, x, yh, yl


def pack_kernel(core, q, tq, k, tk, v, tv, cot, own_kv, sib_kv, sib_q, sems):
    c = core[0]
    mine = pl.multiple_of(c * HALF, HALF)
    other = pl.multiple_of((1 - c) * HALF, HALF)
    copies = []

    def put(source, start, target, entry):
        copy = pltpu.make_async_copy(
            source.at[0, :, pl.ds(start, HALF)], target.at[entry], sems.at[len(copies)]
        )
        copy.start()
        copies.append(copy)

    for entry, source in enumerate((k, tk, v, tv)):
        put(source, mine, own_kv, entry)
    for entry, source in enumerate((k, tk, v, tv)):
        put(source, other, sib_kv, entry)
    for entry, source in enumerate((q, tq)):
        put(source, other, sib_q, entry)
    put(cot, 0, sib_q, 2)
    put(cot, HALF, sib_q, 3)
    for copy in copies:
        copy.wait()


def pack(core, arrays):
    anywhere = pl.BlockSpec(memory_space=pl.ANY)
    four = jax.ShapeDtypeStruct((4, ROWS, HALF), BF16)
    return pl.pallas_call(
        pack_kernel,
        out_shape=(four, four, four),
        in_specs=[pl.BlockSpec(memory_space=pltpu.SMEM)] + [anywhere] * 7,
        out_specs=(anywhere, anywhere, anywhere),
        scratch_shapes=[pltpu.SemaphoreType.DMA((12,))],
        name="pack",
    )(core, *arrays)


def project_kernel(cot, sib_q, weight, out, both):
    @pl.when(pl.program_id(0) == 0)
    def _():
        both[:ROWS, :] = cot[0]
        both[ROWS:, :HALF] = sib_q[0]
        both[ROWS:, HALF:] = sib_q[1]

    out[...] = lax.dot_general(
        both[...], weight[...], (((1,), (1,)), ((), ())), preferred_element_type=F32
    ).astype(BF16)


def project(cot, sib_q, weight):
    tile = 256
    return pl.pallas_call(
        project_kernel,
        grid=(HALF // tile,),
        out_shape=jax.ShapeDtypeStruct((2 * ROWS, HALF), BF16),
        in_specs=[
            pl.BlockSpec((1, ROWS, WIDTH), lambda i: (0, 0, 0)),
            pl.BlockSpec((2, ROWS, HALF), lambda i: (1, 0, 0)),
            pl.BlockSpec((tile, WIDTH), lambda i: (i, 0)),
        ],
        out_specs=pl.BlockSpec((2 * ROWS, tile), lambda i: (0, i)),
        scratch_shapes=[pltpu.VMEM((2 * ROWS, WIDTH), BF16)],
        compiler_params=pltpu.CompilerParams(vmem_limit_bytes=VMEM_LIMIT),
        name="project",
    )(cot, sib_q, weight)


def dot(a, b, dims):
    return lax.dot_general(a, b, (dims, ((), ())), preferred_element_type=F32)


NT = ((1,), (1,))
NN = ((1,), (0,))
TN = ((0,), (0,))


def attend_kernel(
    core, q, tq, k, tk, v, tv, sib_kv, sib_q, far_own, far_sib, grad,
    tan_out, own_out, sib_out, back_own, back_sib,
    keys, values, tvals, queries, grads, prob_all, gs_all, tan_all, qg_all, kg_all, vg_all,
):
    c = core[0]
    mine = pl.multiple_of(c * ROWS, ROWS)
    other = pl.multiple_of((1 - c) * ROWS, ROWS)
    span = 3 * ROWS

    @pl.when(pl.program_id(0) == 0)
    def _():
        zero = jnp.zeros((ROWS, ROWS), BF16)
        for ref in (prob_all, gs_all):
            ref[:ROWS, span:] = zero
            ref[ROWS:, :ROWS] = zero

    def place(start, k_new, tk_new, v_new, tv_new):
        rows = pl.ds(start, ROWS)
        keys[rows, :HEAD_DIM] = k_new
        keys[rows, HEAD_DIM:] = tk_new
        values[rows, :] = v_new
        tvals[rows, :] = tv_new

    place(mine, *(far_own[i] for i in range(4)))
    place(other, *(far_sib[i] for i in range(4)))
    place(2 * ROWS + mine, k[0], tk[0], v[0], tv[0])
    place(2 * ROWS + other, *(sib_kv[i] for i in range(4)))
    queries[pl.ds(mine, ROWS), :HEAD_DIM] = tq[0]
    queries[pl.ds(mine, ROWS), HEAD_DIM:] = q[0]
    queries[pl.ds(other, ROWS), :HEAD_DIM] = sib_q[1]
    queries[pl.ds(other, ROWS), HEAD_DIM:] = sib_q[0]
    grads[pl.ds(mine, ROWS), :] = grad[:ROWS]
    grads[pl.ds(other, ROWS), :] = grad[ROWS:]

    for block in range(2):
        rows = slice(block * ROWS, (block + 1) * ROWS)
        seen = slice(block * ROWS, block * ROWS + span)
        query = queries[rows, :]
        key = keys[seen, :]
        value = values[seen, :]
        scores = dot(query[:, HEAD_DIM:], key[:, :HEAD_DIM], NT) * FACTOR
        tan_scores = dot(query, key, NT) * FACTOR
        grad_prob = dot(grads[rows, :], value, NT)
        top = jnp.max(scores, axis=-1, keepdims=True)
        expos = jnp.exp(scores - top)
        prob = expos * (1.0 / jnp.sum(expos, axis=-1, keepdims=True))
        prob_b = prob.astype(BF16)
        mean = jnp.sum(prob * tan_scores, axis=-1, keepdims=True)
        tan_prob = (prob * (tan_scores - mean)).astype(BF16)
        delta = jnp.sum(prob_b.astype(F32) * grad_prob, axis=-1, keepdims=True)
        gs = (prob * (grad_prob - delta) * FACTOR).astype(BF16)
        tan = dot(prob_b, tvals[seen, :], NN) + dot(tan_prob, value, NN)
        tan_all[rows, :] = tan.astype(BF16)
        qg_all[rows, :] = dot(gs, key[:, :HEAD_DIM], NN)
        prob_all[rows, seen] = prob_b
        gs_all[rows, seen] = gs

    kg_all[...] = dot(gs_all[...], queries[:, HEAD_DIM:], TN)
    vg_all[...] = dot(prob_all[...], grads[...], TN)

    my_rows, other_rows = pl.ds(mine, ROWS), pl.ds(other, ROWS)
    tan_out[:ROWS] = tan_all[my_rows, :]
    tan_out[ROWS:] = tan_all[other_rows, :]
    back_own[0] = kg_all[my_rows, :].astype(BF16)
    back_own[1] = vg_all[my_rows, :].astype(BF16)
    back_sib[0] = kg_all[other_rows, :].astype(BF16)
    back_sib[1] = vg_all[other_rows, :].astype(BF16)
    my_keys, other_keys = pl.ds(2 * ROWS + mine, ROWS), pl.ds(2 * ROWS + other, ROWS)
    own_out[0] = qg_all[my_rows, :]
    own_out[1] = kg_all[my_keys, :]
    own_out[2] = vg_all[my_keys, :]
    sib_out[0] = qg_all[other_rows, :].astype(BF16)
    sib_out[1] = kg_all[other_keys, :].astype(BF16)
    sib_out[2] = vg_all[other_keys, :].astype(BF16)


def attend(core, arrays, sib_kv, sib_q, far_own, far_sib, grad):
    raw = pl.BlockSpec((1, ROWS, HEAD_DIM), lambda h, core: (0, 0, core[0] * HALF_HEADS + h))

    def stack(n):
        return pl.BlockSpec((n, ROWS, HEAD_DIM), lambda h, core: (0, 0, h))

    two = pl.BlockSpec((2 * ROWS, HEAD_DIM), lambda h, core: (0, h))

    def out(n, dtype):
        return jax.ShapeDtypeStruct((n, ROWS, HALF), dtype)

    return pl.pallas_call(
        attend_kernel,
        out_shape=(
            jax.ShapeDtypeStruct((2 * ROWS, HALF), BF16),
            out(3, F32),
            out(3, BF16),
            out(2, BF16),
            out(2, BF16),
        ),
        grid_spec=pltpu.PrefetchScalarGridSpec(
            num_scalar_prefetch=1,
            grid=(HALF_HEADS,),
            in_specs=[raw] * 6 + [stack(4), stack(2), stack(4), stack(4), two],
            out_specs=(two, stack(3), stack(3), stack(2), stack(2)),
            scratch_shapes=[
                pltpu.VMEM((4 * ROWS, 2 * HEAD_DIM), BF16),
                pltpu.VMEM((4 * ROWS, HEAD_DIM), BF16),
                pltpu.VMEM((4 * ROWS, HEAD_DIM), BF16),
                pltpu.VMEM((2 * ROWS, 2 * HEAD_DIM), BF16),
                pltpu.VMEM((2 * ROWS, HEAD_DIM), BF16),
                pltpu.VMEM((2 * ROWS, 4 * ROWS), BF16),
                pltpu.VMEM((2 * ROWS, 4 * ROWS), BF16),
                pltpu.VMEM((2 * ROWS, HEAD_DIM), BF16),
                pltpu.VMEM((2 * ROWS, HEAD_DIM), F32),
                pltpu.VMEM((4 * ROWS, HEAD_DIM), F32),
                pltpu.VMEM((4 * ROWS, HEAD_DIM), F32),
            ],
        ),
        compiler_params=pltpu.CompilerParams(vmem_limit_bytes=VMEM_LIMIT),
        name="attend",
    )(core, *arrays, sib_kv, sib_q, far_own, far_sib, grad)


def tangent_kernel(tan, weight, own, sib):
    both = dot(tan[...], weight[...], NN)
    own[...] = both[:ROWS]
    sib[...] = both[ROWS:].astype(BF16)


def tangent(tan, weight):
    tile = 512
    return pl.pallas_call(
        tangent_kernel,
        grid=(WIDTH // tile,),
        out_shape=(
            jax.ShapeDtypeStruct((ROWS, WIDTH), F32),
            jax.ShapeDtypeStruct((ROWS, WIDTH), BF16),
        ),
        in_specs=[
            pl.BlockSpec((2 * ROWS, HALF), lambda i: (0, 0)),
            pl.BlockSpec((HALF, tile), lambda i: (0, i)),
        ],
        out_specs=(
            pl.BlockSpec((ROWS, tile), lambda i: (0, i)),
            pl.BlockSpec((ROWS, tile), lambda i: (0, i)),
        ),
        compiler_params=pltpu.CompilerParams(vmem_limit_bytes=VMEM_LIMIT),
        name="tangent",
    )(tan, weight)


def finish_first_kernel(core, own, sib, tan_own, tan_sib, q_out, tan_out):
    c = core[0]
    mine = pl.multiple_of(c * HALF, HALF)
    other = pl.multiple_of((1 - c) * HALF, HALF)
    tan_out[0] = (tan_own[...] + tan_sib[...].astype(F32)).astype(BF16)
    q_out[0, :, pl.ds(mine, HALF)] = own[0].astype(BF16)
    q_out[0, :, pl.ds(other, HALF)] = sib[0]


def finish_last_kernel(core, own, sib, near, cross, k_out, v_out):
    c = core[0]
    mine = pl.multiple_of(c * HALF, HALF)
    other = pl.multiple_of((1 - c) * HALF, HALF)
    for entry, ref in enumerate((k_out, v_out)):
        ref[0, :, pl.ds(mine, HALF)] = (own[entry + 1] + near[entry].astype(F32)).astype(BF16)
        ref[0, :, pl.ds(other, HALF)] = (
            sib[entry + 1].astype(F32) + cross[entry].astype(F32)
        ).astype(BF16)


def finish(kernel, name, core, *arrays):
    whole = pl.BlockSpec(memory_space=pltpu.VMEM)
    out = jax.ShapeDtypeStruct((1, ROWS, WIDTH), BF16)
    return pl.pallas_call(
        kernel,
        out_shape=(out, out),
        in_specs=[pl.BlockSpec(memory_space=pltpu.SMEM)] + [whole] * len(arrays),
        out_specs=(whole, whole),
        compiler_params=pltpu.CompilerParams(vmem_limit_bytes=VMEM_LIMIT),
        name=name,
    )(core, *arrays)


def body(q, k, v, tq, tk, tv, cot, out_weight):
    core = lax.axis_index("c").astype(jnp.int32).reshape(1)
    arrays = (q, tq, k, tk, v, tv)

    shard = permute(out_weight, swap_low_and_core)
    weight = lax.all_gather(shard, "z", axis=0, tiled=True)

    own_kv, sib_kv, sib_q = pack(core, arrays + (cot,))
    far_own = permute(own_kv, to_chip(1))
    sib_kv = permute(sib_kv, to_sibling)
    sib_q = permute(sib_q, to_sibling)
    far_sib = permute(sib_kv, to_chip(1))

    grad = project(cot, sib_q, weight)
    tan, own, sib, back_own, back_sib = attend(
        core, arrays, sib_kv, sib_q, far_own, far_sib, grad
    )
    back_own = permute(back_own, to_chip(-1))
    back_sib = permute(back_sib, to_chip(-1, cross=True))
    sib = permute(sib, to_sibling)
    tan_own, tan_sib = tangent(tan, weight)
    tan_sib = permute(tan_sib, to_sibling)
    query_grad, tangent_out = finish(
        finish_first_kernel, "finish_first", core, own, sib, tan_own, tan_sib
    )
    key_grad, value_grad = finish(
        finish_last_kernel, "finish_last", core, own, sib, back_own, back_sib
    )
    return tangent_out, query_grad, key_grad, value_grad


def solution(mesh):
    cut = Mesh(mesh.devices.reshape(SIZES), AXES)
    rows = P(("yl", "z"), ("x", "yh", "c"), None)
    return jax.shard_map(
        body,
        mesh=cut,
        in_specs=(rows,) * 7 + (P(("yl", "z"), None),),
        out_specs=(rows,) * 4,
        check_vma=False,
    )
```

```python
import functools

import jax
import jax.numpy as jnp
from jax import lax
from jax.experimental import pallas as pl
from jax.experimental.pallas import tpu as pltpu
from jax.sharding import Mesh
from jax.sharding import PartitionSpec as P

HEADS = 20
HEAD_DIM = 128
ROWS = 128
WIDTH = HEADS * HEAD_DIM
HALF = WIDTH // 2
HALF_HEADS = HEADS // 2
FACTOR = HEAD_DIM ** (-0.5)

AXES = ("yl", "z", "x", "yh", "c")
SIZES = (2, 8, 4, 2, 2)

F32 = jnp.float32
BF16 = jnp.bfloat16
VMEM_LIMIT = 48 * 1024 * 1024


def permute(block, move):
    route = []
    for index in range(256):
        rest, place = index, []
        for size in reversed(SIZES):
            place.append(rest % size)
            rest //= size
        goal = 0
        for coordinate, size in zip(move(*reversed(place)), SIZES):
            goal = goal * size + coordinate
        route.append((index, goal))
    return lax.ppermute(block, AXES, route)


def to_chip(step, cross=False):
    def move(yl, z, x, yh, c):
        chip = (x * 2 + yh + step) % 8
        return yl, z, chip // 2, chip % 2, (1 - c if cross else c)

    return move


def to_sibling(yl, z, x, yh, c):
    return yl, z, x, yh, 1 - c


def swap_low_and_core(yl, z, x, yh, c):
    return c, z, x, yh, yl


def pack_kernel(core, q, tq, k, tk, v, tv, cot, own_kv, sib_kv, sib_q):
    c = core[0]
    mine = pl.ds(pl.multiple_of(c * HALF, HALF), HALF)
    other = pl.ds(pl.multiple_of((1 - c) * HALF, HALF), HALF)
    for entry, source in enumerate((k, tk, v, tv)):
        own_kv[entry] = source[0, :, mine]
        sib_kv[entry] = source[0, :, other]
    for entry, source in enumerate((q, tq)):
        sib_q[entry] = source[0, :, other]
    sib_q[2] = cot[0, :, :HALF]
    sib_q[3] = cot[0, :, HALF:]


def pack(core, arrays):
    tile = 32
    raw = pl.BlockSpec((1, tile, WIDTH), lambda i: (0, i, 0))
    four = jax.ShapeDtypeStruct((4, ROWS, HALF), BF16)
    out = pl.BlockSpec((4, tile, HALF), lambda i: (0, i, 0))
    return pl.pallas_call(
        pack_kernel,
        grid=(ROWS // tile,),
        out_shape=(four, four, four),
        in_specs=[pl.BlockSpec(memory_space=pltpu.SMEM)] + [raw] * 7,
        out_specs=(out, out, out),
        compiler_params=pltpu.CompilerParams(vmem_limit_bytes=VMEM_LIMIT),
        name="pack",
    )(core, *arrays)


def project_kernel(cot, sib_q, weight, out, both):
    @pl.when(pl.program_id(0) == 0)
    def _():
        both[:ROWS, :] = cot[0]
        both[ROWS:, :HALF] = sib_q[0]
        both[ROWS:, HALF:] = sib_q[1]

    out[...] = lax.dot_general(
        both[...], weight[...], (((1,), (1,)), ((), ())), preferred_element_type=F32
    ).astype(BF16)


def project(cot, sib_q, weight):
    tile = 256
    return pl.pallas_call(
        project_kernel,
        grid=(HALF // tile,),
        out_shape=jax.ShapeDtypeStruct((2 * ROWS, HALF), BF16),
        in_specs=[
            pl.BlockSpec((1, ROWS, WIDTH), lambda i: (0, 0, 0)),
            pl.BlockSpec((2, ROWS, HALF), lambda i: (1, 0, 0)),
            pl.BlockSpec((tile, WIDTH), lambda i: (i, 0)),
        ],
        out_specs=pl.BlockSpec((2 * ROWS, tile), lambda i: (0, i)),
        scratch_shapes=[pltpu.VMEM((2 * ROWS, WIDTH), BF16)],
        compiler_params=pltpu.CompilerParams(vmem_limit_bytes=VMEM_LIMIT),
        name="project",
    )(cot, sib_q, weight)


def dot(a, b, dims):
    return lax.dot_general(a, b, (dims, ((), ())), preferred_element_type=F32)


NT = ((1,), (1,))
NN = ((1,), (0,))
TN = ((0,), (0,))


def attend_kernel(
    core, q, tq, k, tk, v, tv, sib_kv, sib_q, far_own, far_sib, grad,
    tan_out, own_out, sib_out, back_own, back_sib,
    keys, values, tvals, queries, grads, prob_all, gs_all, tan_all, qg_all, kg_all, vg_all,
):
    c = core[0]
    mine = pl.multiple_of(c * ROWS, ROWS)
    other = pl.multiple_of((1 - c) * ROWS, ROWS)
    span = 3 * ROWS

    @pl.when(pl.program_id(0) == 0)
    def _():
        zero = jnp.zeros((ROWS, ROWS), BF16)
        for ref in (prob_all, gs_all):
            ref[:ROWS, span:] = zero
            ref[ROWS:, :ROWS] = zero

    def place(start, k_new, tk_new, v_new, tv_new):
        rows = pl.ds(start, ROWS)
        keys[rows, :HEAD_DIM] = k_new
        keys[rows, HEAD_DIM:] = tk_new
        values[rows, :] = v_new
        tvals[rows, :] = tv_new

    place(mine, *(far_own[i] for i in range(4)))
    place(other, *(far_sib[i] for i in range(4)))
    place(2 * ROWS + mine, k[0], tk[0], v[0], tv[0])
    place(2 * ROWS + other, *(sib_kv[i] for i in range(4)))
    queries[pl.ds(mine, ROWS), :HEAD_DIM] = tq[0]
    queries[pl.ds(mine, ROWS), HEAD_DIM:] = q[0]
    queries[pl.ds(other, ROWS), :HEAD_DIM] = sib_q[1]
    queries[pl.ds(other, ROWS), HEAD_DIM:] = sib_q[0]
    grads[pl.ds(mine, ROWS), :] = grad[:ROWS]
    grads[pl.ds(other, ROWS), :] = grad[ROWS:]

    for block in range(2):
        rows = slice(block * ROWS, (block + 1) * ROWS)
        seen = slice(block * ROWS, block * ROWS + span)
        query = queries[rows, :]
        key = keys[seen, :]
        value = values[seen, :]
        scores = dot(query[:, HEAD_DIM:], key[:, :HEAD_DIM], NT) * FACTOR
        tan_scores = dot(query, key, NT) * FACTOR
        grad_prob = dot(grads[rows, :], value, NT)
        top = jnp.max(scores, axis=-1, keepdims=True)
        expos = jnp.exp(scores - top)
        prob = expos * (1.0 / jnp.sum(expos, axis=-1, keepdims=True))
        prob_b = prob.astype(BF16)
        mean = jnp.sum(prob * tan_scores, axis=-1, keepdims=True)
        tan_prob = (prob * (tan_scores - mean)).astype(BF16)
        delta = jnp.sum(prob_b.astype(F32) * grad_prob, axis=-1, keepdims=True)
        gs = (prob * (grad_prob - delta) * FACTOR).astype(BF16)
        tan = dot(prob_b, tvals[seen, :], NN) + dot(tan_prob, value, NN)
        tan_all[rows, :] = tan.astype(BF16)
        qg_all[rows, :] = dot(gs, key[:, :HEAD_DIM], NN)
        prob_all[rows, seen] = prob_b
        gs_all[rows, seen] = gs

    kg_all[...] = dot(gs_all[...], queries[:, HEAD_DIM:], TN)
    vg_all[...] = dot(prob_all[...], grads[...], TN)

    my_rows, other_rows = pl.ds(mine, ROWS), pl.ds(other, ROWS)
    tan_out[:ROWS] = tan_all[my_rows, :]
    tan_out[ROWS:] = tan_all[other_rows, :]
    back_own[0] = kg_all[my_rows, :].astype(BF16)
    back_own[1] = vg_all[my_rows, :].astype(BF16)
    back_sib[0] = kg_all[other_rows, :].astype(BF16)
    back_sib[1] = vg_all[other_rows, :].astype(BF16)
    my_keys, other_keys = pl.ds(2 * ROWS + mine, ROWS), pl.ds(2 * ROWS + other, ROWS)
    own_out[0] = qg_all[my_rows, :]
    own_out[1] = kg_all[my_keys, :]
    own_out[2] = vg_all[my_keys, :]
    sib_out[0] = qg_all[other_rows, :].astype(BF16)
    sib_out[1] = kg_all[other_keys, :].astype(BF16)
    sib_out[2] = vg_all[other_keys, :].astype(BF16)


def attend(core, arrays, sib_kv, sib_q, far_own, far_sib, grad):
    raw = pl.BlockSpec((1, ROWS, HEAD_DIM), lambda h, core: (0, 0, core[0] * HALF_HEADS + h))

    def stack(n):
        return pl.BlockSpec((n, ROWS, HEAD_DIM), lambda h, core: (0, 0, h))

    two = pl.BlockSpec((2 * ROWS, HEAD_DIM), lambda h, core: (0, h))

    def out(n, dtype):
        return jax.ShapeDtypeStruct((n, ROWS, HALF), dtype)

    return pl.pallas_call(
        attend_kernel,
        out_shape=(
            jax.ShapeDtypeStruct((2 * ROWS, HALF), BF16),
            out(3, F32),
            out(3, BF16),
            out(2, BF16),
            out(2, BF16),
        ),
        grid_spec=pltpu.PrefetchScalarGridSpec(
            num_scalar_prefetch=1,
            grid=(HALF_HEADS,),
            in_specs=[raw] * 6 + [stack(4), stack(2), stack(4), stack(4), two],
            out_specs=(two, stack(3), stack(3), stack(2), stack(2)),
            scratch_shapes=[
                pltpu.VMEM((4 * ROWS, 2 * HEAD_DIM), BF16),
                pltpu.VMEM((4 * ROWS, HEAD_DIM), BF16),
                pltpu.VMEM((4 * ROWS, HEAD_DIM), BF16),
                pltpu.VMEM((2 * ROWS, 2 * HEAD_DIM), BF16),
                pltpu.VMEM((2 * ROWS, HEAD_DIM), BF16),
                pltpu.VMEM((2 * ROWS, 4 * ROWS), BF16),
                pltpu.VMEM((2 * ROWS, 4 * ROWS), BF16),
                pltpu.VMEM((2 * ROWS, HEAD_DIM), BF16),
                pltpu.VMEM((2 * ROWS, HEAD_DIM), F32),
                pltpu.VMEM((4 * ROWS, HEAD_DIM), F32),
                pltpu.VMEM((4 * ROWS, HEAD_DIM), F32),
            ],
        ),
        compiler_params=pltpu.CompilerParams(vmem_limit_bytes=VMEM_LIMIT),
        name="attend",
    )(core, *arrays, sib_kv, sib_q, far_own, far_sib, grad)


def tangent_kernel(tan, weight, own, sib):
    both = dot(tan[...], weight[...], NN)
    own[...] = both[:ROWS]
    sib[...] = both[ROWS:].astype(BF16)


def tangent(tan, weight):
    tile = 512
    return pl.pallas_call(
        tangent_kernel,
        grid=(WIDTH // tile,),
        out_shape=(
            jax.ShapeDtypeStruct((ROWS, WIDTH), F32),
            jax.ShapeDtypeStruct((ROWS, WIDTH), BF16),
        ),
        in_specs=[
            pl.BlockSpec((2 * ROWS, HALF), lambda i: (0, 0)),
            pl.BlockSpec((HALF, tile), lambda i: (0, i)),
        ],
        out_specs=(
            pl.BlockSpec((ROWS, tile), lambda i: (0, i)),
            pl.BlockSpec((ROWS, tile), lambda i: (0, i)),
        ),
        compiler_params=pltpu.CompilerParams(vmem_limit_bytes=VMEM_LIMIT),
        name="tangent",
    )(tan, weight)


def finish_first_kernel(core, own, sib, tan_own, tan_sib, q_out, tan_out):
    c = core[0]
    mine = pl.multiple_of(c * HALF, HALF)
    other = pl.multiple_of((1 - c) * HALF, HALF)
    tan_out[0] = (tan_own[...] + tan_sib[...].astype(F32)).astype(BF16)
    q_out[0, :, pl.ds(mine, HALF)] = own[0].astype(BF16)
    q_out[0, :, pl.ds(other, HALF)] = sib[0]


def finish_last_kernel(core, own, sib, near, cross, k_out, v_out):
    c = core[0]
    mine = pl.multiple_of(c * HALF, HALF)
    other = pl.multiple_of((1 - c) * HALF, HALF)
    for entry, ref in enumerate((k_out, v_out)):
        ref[0, :, pl.ds(mine, HALF)] = (own[entry + 1] + near[entry].astype(F32)).astype(BF16)
        ref[0, :, pl.ds(other, HALF)] = (
            sib[entry + 1].astype(F32) + cross[entry].astype(F32)
        ).astype(BF16)


def finish(kernel, name, core, *arrays):
    whole = pl.BlockSpec(memory_space=pltpu.VMEM)
    out = jax.ShapeDtypeStruct((1, ROWS, WIDTH), BF16)
    return pl.pallas_call(
        kernel,
        out_shape=(out, out),
        in_specs=[pl.BlockSpec(memory_space=pltpu.SMEM)] + [whole] * len(arrays),
        out_specs=(whole, whole),
        compiler_params=pltpu.CompilerParams(vmem_limit_bytes=VMEM_LIMIT),
        name=name,
    )(core, *arrays)


def body(q, k, v, tq, tk, tv, cot, out_weight):
    core = lax.axis_index("c").astype(jnp.int32).reshape(1)
    arrays = (q, tq, k, tk, v, tv)

    shard = permute(out_weight, swap_low_and_core)
    weight = lax.all_gather(shard, "z", axis=0, tiled=True)

    own_kv, sib_kv, sib_q = pack(core, arrays + (cot,))
    far_own = permute(own_kv, to_chip(1))
    sib_kv = permute(sib_kv, to_sibling)
    sib_q = permute(sib_q, to_sibling)
    far_sib = permute(sib_kv, to_chip(1))

    grad = project(cot, sib_q, weight)
    tan, own, sib, back_own, back_sib = attend(
        core, arrays, sib_kv, sib_q, far_own, far_sib, grad
    )
    back_own = permute(back_own, to_chip(-1))
    back_sib = permute(back_sib, to_chip(-1, cross=True))
    sib = permute(sib, to_sibling)
    tan_own, tan_sib = tangent(tan, weight)
    tan_sib = permute(tan_sib, to_sibling)
    query_grad, tangent_out = finish(
        finish_first_kernel, "finish_first", core, own, sib, tan_own, tan_sib
    )
    key_grad, value_grad = finish(
        finish_last_kernel, "finish_last", core, own, sib, back_own, back_sib
    )
    return tangent_out, query_grad, key_grad, value_grad


def solution(mesh):
    cut = Mesh(mesh.devices.reshape(SIZES), AXES)
    rows = P(("yl", "z"), ("x", "yh", "c"), None)
    return jax.shard_map(
        body,
        mesh=cut,
        in_specs=(rows,) * 7 + (P(("yl", "z"), None),),
        out_specs=(rows,) * 4,
        check_vma=False,
    )
```

```python
import jax
import jax.numpy as jnp
from jax import lax
from jax.experimental import pallas as pl
from jax.experimental.pallas import tpu as pltpu
from jax.sharding import Mesh
from jax.sharding import PartitionSpec as P

HEADS = 20
HEAD_DIM = 128
ROWS = 128
WIDTH = HEADS * HEAD_DIM
HALF = WIDTH // 2
PART = WIDTH // 4
PART_HEADS = HEADS // 4
FACTOR = HEAD_DIM ** (-0.5)

AXES = ("yl", "z", "x", "yh", "c")
SIZES = (2, 8, 4, 2, 2)

F32 = jnp.float32
BF16 = jnp.bfloat16
VMEM_LIMIT = 60 * 1024 * 1024
SMALL_LIMIT = 28 * 1024 * 1024
COST = pl.CostEstimate(flops=10**10, bytes_accessed=10**7, transcendentals=0)


def permute(block, move):
    route = []
    for index in range(256):
        rest, place = index, []
        for size in reversed(SIZES):
            place.append(rest % size)
            rest //= size
        goal = 0
        for coordinate, size in zip(move(*reversed(place)), SIZES):
            goal = goal * size + coordinate
        route.append((index, goal))
    return lax.ppermute(block, AXES, route)


def to_chip(step, cross=False):
    def move(yl, z, x, yh, c):
        chip = (x * 2 + yh + step) % 8
        return yl, z, chip // 2, chip % 2, (1 - c if cross else c)

    return move


def to_sibling(yl, z, x, yh, c):
    return yl, z, x, yh, 1 - c


def to_pair(yl, z, x, yh, c):
    return yl, z, x ^ 1, yh, c


def swap_low_and_core(yl, z, x, yh, c):
    return c, z, x, yh, yl


def columns(part, width=PART):
    return pl.ds(pl.multiple_of(part * width, width), width)


def dot(a, b, dims):
    return lax.dot_general(a, b, (dims, ((), ())), preferred_element_type=F32)


NT = ((1,), (1,))
NN = ((1,), (0,))
TN = ((0,), (0,))
ANYWHERE = pl.BlockSpec(memory_space=pl.ANY)
SCALARS = pl.BlockSpec(memory_space=pltpu.SMEM)


def stacked(n):
    return jax.ShapeDtypeStruct((n, ROWS, PART), BF16)


def pack_call(kernel, name, inputs, outputs, *arrays):
    steps = 2
    tile = ROWS // steps

    def spec(n):
        if n is None:
            return ANYWHERE
        if n == 0:
            return pl.BlockSpec((1, tile, WIDTH), lambda i: (0, i, 0))
        return pl.BlockSpec((n, tile, PART), lambda i: (0, i, 0))

    return pl.pallas_call(
        kernel,
        grid=(steps,),
        out_shape=[stacked(n) for n in outputs],
        in_specs=[SCALARS] + [spec(n) for n in inputs],
        out_specs=[spec(n) for n in outputs],
        compiler_params=pltpu.CompilerParams(vmem_limit_bytes=VMEM_LIMIT),
        cost_estimate=COST,
        name=name,
    )(*arrays)


def pack_first_kernel(place, q, tq, k, tk, v, tv, cot, own, sib, pair):
    core, side = place[0], place[1]
    for entry, source in enumerate((k, tk, v, tv, q, tq)):
        if entry < 4:
            own[entry] = source[0, :, columns(2 * core)]
        sib[entry] = source[0, :, columns(2 - 2 * core)]
    for entry, source in enumerate((q, tq)):
        sib[6 + entry] = source[0, :, columns(3 - 2 * core)]
    for entry in range(2):
        sib[8 + entry] = cot[0, :, columns(2 * side + entry)]
        pair[entry] = cot[0, :, columns(2 - 2 * side + entry)]


def pack_second_kernel(place, k, tk, v, tv, near, far, sib):
    core = place[0]
    for entry, source in enumerate((k, tk, v, tv)):
        far[entry] = near[entry]
        far[4 + entry] = source[0, :, columns(2 * core + 1)]
        sib[entry] = source[0, :, columns(3 - 2 * core)]


def halves_kernel(place, shard, first, used, other):
    del first
    side = place[1]
    used[...] = shard[:, columns(side, HALF)]
    other[...] = shard[:, columns(1 - side, HALF)]


def halves(place, shard, first):
    whole = pl.BlockSpec(memory_space=pltpu.VMEM)
    out = jax.ShapeDtypeStruct((shard.shape[0], HALF), BF16)
    return pl.pallas_call(
        halves_kernel,
        out_shape=(out, out),
        in_specs=[SCALARS, whole, ANYWHERE],
        out_specs=(whole, whole),
        compiler_params=pltpu.CompilerParams(vmem_limit_bytes=SMALL_LIMIT),
        cost_estimate=COST,
        name="halves",
    )(place, shard, first)


def project_kernel(place, cot, near, pair, pair_near, weight, own, send0, send1, rows):
    del place
    step = pl.program_id(0)

    @pl.when(step == 0)
    def _():
        rows[:ROWS, :] = cot[0]
        for block, ref in enumerate((near, pair, pair_near)):
            start = (block + 1) * ROWS
            rows[start : start + ROWS, :PART] = ref[0]
            rows[start : start + ROWS, PART:] = ref[1]

    out = dot(rows[...], weight[...], NT)
    own[...] = out[: 2 * ROWS]
    for chunk, send in enumerate((send0, send1)):

        @pl.when(step == chunk)
        def _(send=send):
            send[...] = out[2 * ROWS :].astype(BF16)


def project(place, cot, near, pair, pair_near, weight):
    def stack(start):
        return pl.BlockSpec((2, ROWS, PART), lambda i, place: (start, 0, 0))

    block = pl.BlockSpec((2 * ROWS, PART), lambda i, place: (0, 0))
    send = jax.ShapeDtypeStruct((2 * ROWS, PART), BF16)
    return pl.pallas_call(
        project_kernel,
        out_shape=(jax.ShapeDtypeStruct((2 * ROWS, HALF), F32), send, send),
        grid_spec=pltpu.PrefetchScalarGridSpec(
            num_scalar_prefetch=1,
            grid=(2,),
            in_specs=[
                pl.BlockSpec((1, ROWS, HALF), lambda i, place: (0, 0, place[1])),
                stack(4),
                stack(0),
                stack(0),
                pl.BlockSpec((PART, HALF), lambda i, place: (i, 0)),
            ],
            out_specs=(
                pl.BlockSpec((2 * ROWS, PART), lambda i, place: (0, i)), block, block
            ),
            scratch_shapes=[pltpu.VMEM((4 * ROWS, HALF), BF16)],
        ),
        compiler_params=pltpu.CompilerParams(vmem_limit_bytes=SMALL_LIMIT),
        cost_estimate=COST,
        name="project",
    )(place, cot, near, pair, pair_near, weight)


def attend_head(core, chunk, head, refs):
    q, tq, k, tk, v, tv, near, near_q, far_own, far_sib, grad_own, grad_pair, *outs = refs
    own_q, own_kv, sib_out, back_own, back_sib, tan_out = outs
    start = head * HEAD_DIM
    cols = slice(start, start + HEAD_DIM)
    start += chunk * PART
    grad_cols = slice(start, start + HEAD_DIM)
    start += core * HALF
    raw = slice(start, start + HEAD_DIM)
    far_entry = 4 * chunk
    sib_far = 4 if chunk == 0 else 4

    def ordered(own, sib):
        return [own, sib] if core == 0 else [sib, own]

    def window(entry, source):
        blocks = ordered(far_own[far_entry + entry, :, cols], far_sib[entry, :, cols]) + ordered(
            source[0, :, raw], near[entry, :, cols]
        )
        return jnp.concatenate(blocks, axis=0)

    key, tkey, value, tvalue = (window(i, source) for i, source in enumerate((k, tk, v, tv)))
    query = ordered(q[0, :, raw], near_q[4 + 2 * chunk, :, cols])
    tquery = ordered(tq[0, :, raw], near_q[5 + 2 * chunk, :, cols])
    grad = (grad_own[:, grad_cols] + grad_pair[:, cols].astype(F32)).astype(BF16)
    grad = ordered(grad[:ROWS], grad[ROWS:])
    both_key = jnp.concatenate([key, tkey], axis=1)
    span = 3 * ROWS
    zero = jnp.zeros((ROWS, ROWS), BF16)
    probs, gss, tans, qgs = [], [], [], []
    for block in range(2):
        seen = slice(block * ROWS, block * ROWS + span)
        scores = dot(query[block], key[seen], NT)
        both_query = jnp.concatenate([tquery[block], query[block]], axis=1)
        tan_scores = dot(both_query, both_key[seen], NT)
        grad_prob = dot(grad[block], value[seen], NT)
        top = jnp.max(scores, axis=-1, keepdims=True)
        expos = jnp.exp((scores - top) * FACTOR)
        prob = expos * (1.0 / jnp.sum(expos, axis=-1, keepdims=True))
        prob_b = prob.astype(BF16)
        mean = jnp.sum(prob * tan_scores, axis=-1, keepdims=True)
        scaled = prob * FACTOR
        tan_prob = (scaled * (tan_scores - mean)).astype(BF16)
        delta = jnp.sum(prob_b.astype(F32) * grad_prob, axis=-1, keepdims=True)
        gs = (scaled * (grad_prob - delta)).astype(BF16)
        tans.append(dot(prob_b, tvalue[seen], NN) + dot(tan_prob, value[seen], NN))
        qgs.append(dot(gs, key[seen], NN))
        fill = [prob_b, zero] if block == 0 else [zero, prob_b]
        probs.append(jnp.concatenate(fill, axis=1))
        fill = [gs, zero] if block == 0 else [zero, gs]
        gss.append(jnp.concatenate(fill, axis=1))
    kg = dot(jnp.concatenate(gss, axis=0), jnp.concatenate(query, axis=0), TN)
    vg = dot(jnp.concatenate(probs, axis=0), jnp.concatenate(grad, axis=0), TN)

    def block_of(whole, index):
        return whole[index * ROWS : (index + 1) * ROWS]

    tan_out[:ROWS, cols] = tans[core].astype(BF16)
    tan_out[ROWS:, cols] = tans[1 - core].astype(BF16)
    own_q[0, :, cols] = qgs[core].astype(BF16)
    sib_out[0, :, cols] = qgs[1 - core].astype(BF16)
    for entry, terms in enumerate((kg, vg)):
        back_own[entry, :, cols] = block_of(terms, core).astype(BF16)
        back_sib[entry, :, cols] = block_of(terms, 1 - core).astype(BF16)
        own_kv[entry, :, cols] = block_of(terms, 2 + core)
        sib_out[1 + entry, :, cols] = block_of(terms, 3 - core).astype(BF16)


def attend(place, chunk, *arrays):
    def kernel(place, *refs):
        for core in range(2):

            @pl.when(place[0] == core)
            def _(core=core):
                for head in range(PART_HEADS):
                    attend_head(core, chunk, head, refs)

    whole = pl.BlockSpec(memory_space=pltpu.VMEM)

    def out(n, dtype):
        return jax.ShapeDtypeStruct((n, ROWS, PART), dtype)

    return pl.pallas_call(
        kernel,
        out_shape=(
            out(1, BF16), out(2, F32), out(3, BF16), out(2, BF16), out(2, BF16),
            jax.ShapeDtypeStruct((2 * ROWS, PART), BF16),
        ),
        in_specs=[SCALARS] + [whole] * len(arrays),
        out_specs=(whole,) * 6,
        compiler_params=pltpu.CompilerParams(vmem_limit_bytes=SMALL_LIMIT),
        cost_estimate=COST,
        name="attend",
    )(place, *arrays)


def tangent_kernel(place, tan0, tan1, weight0, weight1, back, cross, near, own, sib, total):
    del place, back, cross, near
    step = pl.program_id(0)
    for half, weight in enumerate((weight0, weight1)):

        @pl.when(step == 2 * half)
        def _(weight=weight):
            total[...] = dot(tan0[...], weight[...], NN)

        @pl.when(step == 2 * half + 1)
        def _(weight=weight):
            both = total[...] + dot(tan1[...], weight[...], NN)
            own[0] = both[:ROWS]
            sib[0] = both[ROWS:].astype(BF16)


def tangent(place, tan0, tan1, weight0, weight1, *earlier):
    whole = pl.BlockSpec((2 * ROWS, PART), lambda i, place: (0, 0))
    block = pl.BlockSpec((1, ROWS, HALF), lambda i, place: (i // 2, 0, 0))
    return pl.pallas_call(
        tangent_kernel,
        out_shape=(
            jax.ShapeDtypeStruct((2, ROWS, HALF), F32),
            jax.ShapeDtypeStruct((2, ROWS, HALF), BF16),
        ),
        grid_spec=pltpu.PrefetchScalarGridSpec(
            num_scalar_prefetch=1,
            grid=(4,),
            in_specs=[
                whole,
                whole,
                pl.BlockSpec((PART, HALF), lambda i, place: (jnp.minimum(i, 1), 0)),
                pl.BlockSpec((PART, HALF), lambda i, place: (jnp.maximum(i, 2) - 2, 0)),
            ]
            + [ANYWHERE] * len(earlier),
            out_specs=(block, block),
            scratch_shapes=[pltpu.VMEM((2 * ROWS, HALF), F32)],
        ),
        compiler_params=pltpu.CompilerParams(vmem_limit_bytes=SMALL_LIMIT),
        cost_estimate=COST,
        name="tangent",
    )(place, tan0, tan1, weight0, weight1, *earlier)


def finish_first_kernel(place, own0, own1, sib0, sib1, tan_own, tan_sib, q_out, tan_out):
    core, side = place[0], place[1]
    for chunk, (own, sib) in enumerate(((own0, sib0), (own1, sib1))):
        q_out[0, :, columns(2 * core + chunk)] = own[0]
        q_out[0, :, columns(2 - 2 * core + chunk)] = sib[0]
    for entry, half in enumerate((side, 1 - side)):
        tan_out[0, :, columns(half, HALF)] = (
            tan_own[entry] + tan_sib[entry].astype(F32)
        ).astype(BF16)


def finish_last_kernel(
    place, own0, own1, sib0, sib1, near0, near1, cross0, cross1, k_out, v_out
):
    core = place[0]
    chunks = ((own0, sib0, near0, cross0), (own1, sib1, near1, cross1))
    for chunk, (own, sib, near, cross) in enumerate(chunks):
        for entry, ref in enumerate((k_out, v_out)):
            ref[0, :, columns(2 * core + chunk)] = (
                own[entry] + near[entry].astype(F32)
            ).astype(BF16)
            ref[0, :, columns(2 - 2 * core + chunk)] = (
                sib[entry + 1].astype(F32) + cross[entry].astype(F32)
            ).astype(BF16)


def finish(kernel, name, place, *arrays):
    whole = pl.BlockSpec(memory_space=pltpu.VMEM)
    out = jax.ShapeDtypeStruct((1, ROWS, WIDTH), BF16)
    return pl.pallas_call(
        kernel,
        out_shape=(out, out),
        in_specs=[SCALARS] + [whole] * len(arrays),
        out_specs=(whole, whole),
        compiler_params=pltpu.CompilerParams(vmem_limit_bytes=SMALL_LIMIT),
        cost_estimate=COST,
        name=name,
    )(place, *arrays)


def body(q, k, v, tq, tk, tv, cot, out_weight):
    place = jnp.stack([lax.axis_index("c"), lax.axis_index("x") % 2]).astype(jnp.int32)
    arrays = (q, tq, k, tk, v, tv)

    shard = permute(out_weight, swap_low_and_core)
    own, sib, pair = pack_call(
        pack_first_kernel, "pack_first", [0] * 7, [4, 10, 2], place, *arrays, cot
    )
    near_0 = permute(sib, to_sibling)
    far_a = permute(own, to_chip(1))
    pair = permute(pair, to_pair)
    weight_a, weight_b = (
        lax.all_gather(half, "z", axis=0, tiled=True) for half in halves(place, shard, near_0)
    )
    far, sib = pack_call(
        pack_second_kernel, "pack_second", [0] * 4 + [10], [8, 4], place, k, tk, v, tv, near_0
    )
    near_1 = permute(sib, to_sibling)
    far_b = permute(far, to_chip(1))
    far_c = permute(near_1, to_chip(1))
    pair_near = permute(pair, to_sibling)

    grad, send_0, send_1 = project(place, cot, near_0, pair, pair_near, weight_a)
    grad_0 = permute(send_0, to_pair)
    grad_1 = permute(send_1, to_pair)

    def chunk_grads(chunk, *others):
        own_q, own_kv, sib, back_own, back_sib, tan = attend(place, chunk, *arrays, *others)
        back_own = permute(back_own, to_chip(-1))
        back_sib = permute(back_sib, to_chip(-1, cross=True))
        return own_q, own_kv, permute(sib, to_sibling), back_own, back_sib, tan

    q0, kv0, sib0, back0, cross0, tan0 = chunk_grads(
        0, near_0, near_0, far_a, far_b, grad, grad_0
    )
    q1, kv1, sib1, back1, cross1, tan1 = chunk_grads(
        1, near_1, near_0, far_b, far_c, grad, grad_1
    )
    tan_own, tan_sib = tangent(
        place, tan0, tan1, weight_a, weight_b, back0, cross0, sib0
    )
    tan_sib = permute(tan_sib, to_sibling)
    query_grad, tangent_out = finish(
        finish_first_kernel, "finish_first", place, q0, q1, sib0, sib1, tan_own, tan_sib
    )
    key_grad, value_grad = finish(
        finish_last_kernel, "finish_last", place,
        kv0, kv1, sib0, sib1, back0, back1, cross0, cross1,
    )
    return tangent_out, query_grad, key_grad, value_grad


def solution(mesh):
    cut = Mesh(mesh.devices.reshape(SIZES), AXES)
    rows = P(("yl", "z"), ("x", "yh", "c"), None)
    return jax.shard_map(
        body,
        mesh=cut,
        in_specs=(rows,) * 7 + (P(("yl", "z"), None),),
        out_specs=(rows,) * 4,
        check_vma=False,
    )
```

```python
import jax
import jax.numpy as jnp
from jax import lax
from jax.experimental import pallas as pl
from jax.experimental.pallas import tpu as pltpu
from jax.sharding import Mesh
from jax.sharding import PartitionSpec as P

HEADS = 20
HEAD_DIM = 128
ROWS = 128
WIDTH = HEADS * HEAD_DIM
HALF = WIDTH // 2
PART = WIDTH // 4
PART_HEADS = HEADS // 4
FACTOR = HEAD_DIM ** (-0.5)

AXES = ("yl", "z", "x", "yh", "c")
SIZES = (2, 8, 4, 2, 2)

F32 = jnp.float32
BF16 = jnp.bfloat16
VMEM_LIMIT = 63 * 1024 * 1024
COST = pl.CostEstimate(flops=10**10, bytes_accessed=10**7, transcendentals=0)
BIG_COST = pl.CostEstimate(flops=4 * 10**10, bytes_accessed=4 * 10**7, transcendentals=0)
NO_COST = pl.CostEstimate(flops=1, bytes_accessed=1, transcendentals=0)


def permute(block, move):
    route = []
    for index in range(256):
        rest, place = index, []
        for size in reversed(SIZES):
            place.append(rest % size)
            rest //= size
        goal = 0
        for coordinate, size in zip(move(*reversed(place)), SIZES):
            goal = goal * size + coordinate
        route.append((index, goal))
    return lax.ppermute(block, AXES, route)


def to_chip(step, cross=False):
    def move(yl, z, x, yh, c):
        chip = (x * 2 + yh + step) % 8
        return yl, z, chip // 2, chip % 2, (1 - c if cross else c)

    return move


def to_sibling(yl, z, x, yh, c):
    return yl, z, x, yh, 1 - c


def to_pair(yl, z, x, yh, c):
    return yl, z, x ^ 1, yh, c


def swap_low_and_core(yl, z, x, yh, c):
    return c, z, x, yh, yl


def columns(part, width=PART):
    return pl.ds(pl.multiple_of(part * width, width), width)


def dot(a, b, dims):
    return lax.dot_general(a, b, (dims, ((), ())), preferred_element_type=F32)


NT = ((1,), (1,))
NN = ((1,), (0,))
TN = ((0,), (0,))
ANYWHERE = pl.BlockSpec(memory_space=pl.ANY)
SCALARS = pl.BlockSpec(memory_space=pltpu.SMEM)


def stacked(n):
    return jax.ShapeDtypeStruct((n, ROWS, PART), BF16)


def pack_call(kernel, name, inputs, outputs, *arrays):
    steps = 2
    tile = ROWS // steps

    def spec(n):
        if n is None:
            return ANYWHERE
        if n == 0:
            return pl.BlockSpec((1, tile, WIDTH), lambda i: (0, i, 0))
        return pl.BlockSpec((n, tile, PART), lambda i: (0, i, 0))

    return pl.pallas_call(
        kernel,
        grid=(steps,),
        out_shape=[stacked(n) for n in outputs],
        in_specs=[SCALARS] + [spec(n) for n in inputs],
        out_specs=[spec(n) for n in outputs],
        compiler_params=pltpu.CompilerParams(vmem_limit_bytes=VMEM_LIMIT),
        cost_estimate=NO_COST,
        name=name,
    )(*arrays)


def pack_first_kernel(place, q, tq, k, tk, v, tv, cot, sib_kv, sib_q):
    core, side = place[0], place[1]
    for chunk in range(2):
        other = columns(2 - 2 * core + chunk)
        for entry, source in enumerate((k, v, tk, tv)):
            sib_kv[4 * chunk + entry] = source[0, :, other]
        for entry, source in enumerate((q, tq)):
            sib_q[2 * chunk + entry] = source[0, :, other]
    for entry in range(2):
        sib_q[4 + entry] = cot[0, :, columns(2 * side + entry)]


def pack_halo_kernel(place, k, tk, v, tv, near, first, second, far):
    del first, second
    for chunk in range(2):
        mine = columns(2 * place[0] + chunk)
        for entry, source in enumerate((k, v, tk, tv)):
            far[8 * chunk + entry] = source[0, :, mine]
            far[8 * chunk + 4 + entry] = near[4 * chunk + entry]


RING = 8
TO_RIGHT, TO_LEFT = 4, 3


def ring(shard):
    def step(distance):
        return lambda yl, z, x, yh, c: (yl, (z + distance) % RING, x, yh, c)

    right, left = [shard], [shard]
    for index in range(TO_RIGHT):
        right.append(permute(right[-1], step(1)))
        if index < TO_LEFT:
            left.append(permute(left[-1], step(-1)))
    return right + left[1:]


def put_in_order(place, pieces, rows):
    z = place[2]
    depth = HALF // RING
    for index, piece in enumerate(pieces):
        source = z - index if index <= TO_RIGHT else z + index - TO_RIGHT
        start = pl.multiple_of(lax.rem(source + RING, RING) * depth, depth)
        rows[pl.ds(start, depth), :] = piece[...]


def project_kernel(place, cot, near, pair, pair_near, *refs):
    pieces, (own, send, rows, weight) = refs[:RING], refs[RING:]
    put_in_order(place, pieces, weight)
    rows[:ROWS, :] = cot[0]
    rows[ROWS : 2 * ROWS, :PART] = near[0]
    rows[ROWS : 2 * ROWS, PART:] = near[1]
    rows[2 * ROWS : 3 * ROWS, :] = pair[...]
    rows[3 * ROWS :, :] = pair_near[...]
    for chunk in range(2):
        heads = slice(chunk * PART, (chunk + 1) * PART)
        out = dot(rows[...], weight[heads, :], NT)
        own[:, heads] = out[: 2 * ROWS]
        send[chunk] = out[2 * ROWS :].astype(BF16)


def project(place, cot, near, pair, pair_near, pieces):
    def block(rows, width):
        return pl.BlockSpec((rows, width), lambda i, place: (0, 0))

    send = jax.ShapeDtypeStruct((2, 2 * ROWS, PART), BF16)
    return pl.pallas_call(
        project_kernel,
        out_shape=(jax.ShapeDtypeStruct((2 * ROWS, HALF), F32), send),
        grid_spec=pltpu.PrefetchScalarGridSpec(
            num_scalar_prefetch=1,
            grid=(1,),
            in_specs=[
                pl.BlockSpec((1, ROWS, HALF), lambda i, place: (0, 0, place[1])),
                pl.BlockSpec((2, ROWS, PART), lambda i, place: (2, 0, 0)),
                block(ROWS, HALF),
                block(ROWS, HALF),
            ]
            + [block(HALF // RING, HALF)] * RING,
            out_specs=(
                block(2 * ROWS, HALF),
                pl.BlockSpec((2, 2 * ROWS, PART), lambda i, place: (0, 0, 0)),
            ),
            scratch_shapes=[
                pltpu.VMEM((4 * ROWS, HALF), BF16),
                pltpu.VMEM((HALF, HALF), BF16),
            ],
        ),
        compiler_params=pltpu.CompilerParams(vmem_limit_bytes=VMEM_LIMIT),
        cost_estimate=NO_COST,
        name="project",
    )(place, cot, near, pair, pair_near, *pieces)


def ordered(core, own, sib):
    return [own, sib] if core == 0 else [sib, own]


def window(core, cols, source, near, far_own, far_sib):
    blocks = ordered(core, far_own[:, cols], far_sib[:, cols])
    blocks += ordered(core, source[:, cols], near[:, cols])
    return jnp.concatenate(blocks, axis=0)


def probabilities(query, key):
    scores = dot(query, key, NT)
    top = jnp.max(scores, axis=-1, keepdims=True)
    expos = jnp.exp((scores - top) * FACTOR)
    return expos * (1.0 / jnp.sum(expos, axis=-1, keepdims=True))


def tangents_head(core, cols, refs):
    q, tq, k, tk, v, tv, near, near_q, far_own, far_sib, tan_out = refs
    key, value, tkey, tvalue = (
        window(core, cols, source.at[0], near.at[i], far_own.at[i], far_sib.at[i])
        for i, source in enumerate((k, v, tk, tv))
    )
    query = ordered(core, q[0, :, cols], near_q[0, :, cols])
    tquery = ordered(core, tq[0, :, cols], near_q[1, :, cols])
    both_key = jnp.concatenate([key, tkey], axis=1)
    for block in range(2):
        seen = slice(block * ROWS, (block + 3) * ROWS)
        prob = probabilities(query[block], key[seen])
        both_query = jnp.concatenate([tquery[block], query[block]], axis=1)
        tan_scores = dot(both_query, both_key[seen], NT)
        mean = jnp.sum(prob * tan_scores, axis=-1, keepdims=True)
        tan_prob = (prob * FACTOR * (tan_scores - mean)).astype(BF16)
        tan = dot(prob.astype(BF16), tvalue[seen], NN) + dot(tan_prob, value[seen], NN)
        start = 0 if block == core else ROWS
        tan_out[start : start + ROWS, cols] = tan.astype(BF16)


def gradients_head(core, cols, refs):
    q, k, v, near, near_q, far_own, far_sib, grad_own, grad_pair, *outs = refs
    own_q, own_kv, sib, back_own = outs[:4]
    back_sib = back_own.at[2:] if len(outs) == 4 else outs[4]
    key, value = (
        window(core, cols, source.at[0], near.at[i], far_own.at[i], far_sib.at[i])
        for i, source in enumerate((k, v))
    )
    query = ordered(core, q[0, :, cols], near_q[0, :, cols])
    grad = (grad_own[:, cols] + grad_pair[0, :, cols].astype(F32)).astype(BF16)
    grad = ordered(core, grad[:ROWS], grad[ROWS:])
    zero = jnp.zeros((ROWS, ROWS), BF16)
    probs, gss = [], []
    for block in range(2):
        seen = slice(block * ROWS, (block + 3) * ROWS)
        prob = probabilities(query[block], key[seen])
        prob_b = prob.astype(BF16)
        grad_prob = dot(grad[block], value[seen], NT)
        delta = jnp.sum(prob_b.astype(F32) * grad_prob, axis=-1, keepdims=True)
        gs = (prob * FACTOR * (grad_prob - delta)).astype(BF16)
        target, entry = (own_q, 0) if block == core else (sib, 2)
        target[entry, :, cols] = dot(gs, key[seen], NN).astype(BF16)
        for whole, part in ((probs, prob_b), (gss, gs)):
            whole.append(jnp.concatenate([part, zero] if block == 0 else [zero, part], axis=1))
    kg = dot(jnp.concatenate(gss, axis=0), jnp.concatenate(query, axis=0), TN)
    vg = dot(jnp.concatenate(probs, axis=0), jnp.concatenate(grad, axis=0), TN)
    for entry, terms in enumerate((kg, vg)):
        blocks = [terms[i * ROWS : (i + 1) * ROWS] for i in range(4)]
        back_own[entry, :, cols] = blocks[core].astype(BF16)
        back_sib[entry, :, cols] = blocks[1 - core].astype(BF16)
        own_kv[entry, :, cols] = blocks[2 + core]
        sib[entry, :, cols] = blocks[3 - core].astype(BF16)


def by_heads(head_kernel, n_inputs):
    def kernel(place, *refs):
        refs = refs[:n_inputs] + refs[n_inputs + 1 :]
        for core in range(2):

            @pl.when(place[0] == core)
            def _(core=core):
                for head in range(PART_HEADS):
                    head_kernel(core, slice(head * HEAD_DIM, (head + 1) * HEAD_DIM), refs)

    return kernel


def attention_call(kernel, name, grid, in_specs, outputs, cost, *arrays):
    return pl.pallas_call(
        kernel,
        out_shape=[shape for shape, _ in outputs],
        grid_spec=pltpu.PrefetchScalarGridSpec(
            num_scalar_prefetch=1,
            grid=grid,
            in_specs=in_specs + [ANYWHERE],
            out_specs=[spec for _, spec in outputs],
        ),
        compiler_params=pltpu.CompilerParams(vmem_limit_bytes=VMEM_LIMIT),
        cost_estimate=cost,
        name=name,
    )(*arrays)


def tangents(place, arrays, near, near_q, far, first):
    raw = pl.BlockSpec((1, ROWS, PART), lambda i, place: (0, 0, 2 * place[0] + i))

    def stack(n, index):
        return pl.BlockSpec((n, ROWS, PART), lambda i, place: (index(i), 0, 0))

    return attention_call(
        by_heads(tangents_head, 10), "tangents", (2,),
        [raw] * 6
        + [stack(4, lambda i: i), stack(2, lambda i: i)]
        + [stack(4, lambda i: 2 * i), stack(4, lambda i: 2 * i + 1)],
        [(
            jax.ShapeDtypeStruct((2 * ROWS, HALF), BF16),
            pl.BlockSpec((2 * ROWS, PART), lambda i, place: (0, i)),
        )],
        NO_COST, place, *arrays, near, near_q, far, far, first,
    )[0]


def gradients(place, chunk, q, k, v, near, near_q, far, grad, grad_pair, first):
    raw = pl.BlockSpec((1, ROWS, PART), lambda i, place: (0, 0, 2 * place[0] + chunk))

    def stack(n, index):
        return pl.BlockSpec((n, ROWS, PART), lambda i, place: (index, 0, 0))

    def out(n, dtype):
        return jax.ShapeDtypeStruct((n, ROWS, PART), dtype), stack(n, 0)

    return attention_call(
        by_heads(gradients_head, 9), "gradients", (1,),
        [raw] * 3
        + [stack(2, 2 * chunk), stack(1, 2 * chunk), stack(2, 4 * chunk), stack(2, 4 * chunk + 2)]
        + [pl.BlockSpec((2 * ROWS, PART), lambda i, place: (0, chunk))]
        + [pl.BlockSpec((1, 2 * ROWS, PART), lambda i, place: (chunk, 0, 0))],
        [out(1, BF16), out(2, F32), out(3, BF16)]
        + ([out(4, BF16)] if chunk == 0 else [out(2, BF16), out(2, BF16)]),
        NO_COST, place, q, k, v, near, near_q, far, far, grad, grad_pair, first,
    )


def total_first_kernel(own, sib0, sib1, tan_sib, back, first, own_out, sib_out):
    del first
    own_out[...] = (own[...] + back[:2].astype(F32)).astype(BF16)
    sib_out[:2] = (sib0[:2].astype(F32) + back[2:].astype(F32)).astype(BF16)
    sib_out[2] = sib0[2]
    sib_out[3:6] = sib1[...]
    sib_out[6] = tan_sib[:, :PART]
    sib_out[7] = tan_sib[:, PART:]


def total_last_kernel(own, back, cross, own_out, cross_out):
    own_out[...] = (own[...] + back[...].astype(F32)).astype(BF16)
    cross_out[...] = cross[...]


def total(kernel, name, outputs, cost, *arrays, first=()):
    whole = pl.BlockSpec(memory_space=pltpu.VMEM)
    return pl.pallas_call(
        kernel,
        out_shape=[stacked(n) for n in outputs],
        in_specs=[whole] * len(arrays) + [ANYWHERE] * len(first),
        out_specs=[whole] * len(outputs),
        compiler_params=pltpu.CompilerParams(vmem_limit_bytes=VMEM_LIMIT),
        cost_estimate=cost,
        name=name,
    )(*arrays, *first)


def tangent_kernel(place, tan, tan_pair, *refs):
    pieces, (own, pair, own_sib, pair_sib, weight) = refs[:RING], refs[-5:]
    put_in_order(place, pieces, weight)
    for ref, kept, sib in ((tan, own, own_sib), (tan_pair, pair, pair_sib)):
        both = dot(ref[...], weight[...], NN)
        kept[...] = both[:ROWS]
        sib[...] = both[ROWS:].astype(BF16)


def tangent(place, tan, tan_pair, pieces, *first):
    def block(rows, width):
        return pl.BlockSpec((rows, width), lambda i, place: (0, 0))

    kept = jax.ShapeDtypeStruct((ROWS, HALF), F32)
    sent = jax.ShapeDtypeStruct((ROWS, HALF), BF16)
    return pl.pallas_call(
        tangent_kernel,
        out_shape=(kept, kept, sent, sent),
        grid_spec=pltpu.PrefetchScalarGridSpec(
            num_scalar_prefetch=1,
            grid=(1,),
            in_specs=[block(2 * ROWS, HALF)] * 2 + [block(HALF // RING, HALF)] * RING
            + [ANYWHERE] * len(first),
            out_specs=(block(ROWS, HALF),) * 4,
            scratch_shapes=[pltpu.VMEM((HALF, HALF), BF16)],
        ),
        compiler_params=pltpu.CompilerParams(vmem_limit_bytes=VMEM_LIMIT),
        cost_estimate=NO_COST,
        name="tangent",
    )(place, tan, tan_pair, *pieces, *first)


def add_kernel(own, near, *refs):
    out = refs[-1]
    out[...] = (own[...] + near[...].astype(F32)).astype(BF16)


def add(own, near, *first):
    def block(rows, width):
        return pl.BlockSpec((rows, width), lambda i: (0, 0))

    return pl.pallas_call(
        add_kernel,
        grid=(1,),
        out_shape=jax.ShapeDtypeStruct((ROWS, HALF), BF16),
        in_specs=[block(ROWS, HALF), block(ROWS, HALF)]
        + [ANYWHERE] * len(first),
        out_specs=block(ROWS, HALF),
        compiler_params=pltpu.CompilerParams(vmem_limit_bytes=VMEM_LIMIT),
        cost_estimate=NO_COST,
        name="add",
    )(own, near, *first)


def finish_kernel(
    place, q0, q1, own0, own1, sib, cross, tan_own, tan_pair, tan_out, q_out, k_out, v_out
):
    core, side = place[0], place[1]
    for entry in range(2):
        cols = slice(entry * PART, (entry + 1) * PART)
        tan_out[0, :, columns(2 * side + entry)] = (
            tan_own[:, cols] + sib[6 + entry].astype(F32)
        ).astype(BF16)
    tan_out[0, :, columns(1 - side, HALF)] = tan_pair[...]
    for chunk, (q, own) in enumerate(((q0, own0), (q1, own1))):
        mine, other = columns(2 * core + chunk), columns(2 - 2 * core + chunk)
        q_out[0, :, mine] = q[0]
        q_out[0, :, other] = sib[3 * chunk + 2]
        for entry, ref in enumerate((k_out, v_out)):
            term = sib[3 * chunk + entry]
            if chunk == 1:
                term = (term.astype(F32) + cross[entry].astype(F32)).astype(BF16)
            ref[0, :, mine] = own[entry]
            ref[0, :, other] = term


def finish(place, *arrays):
    steps = 2
    tile = ROWS // steps

    def spec(array):
        if array.ndim == 2:
            return pl.BlockSpec((tile, array.shape[1]), lambda i: (i, 0))
        return pl.BlockSpec((array.shape[0], tile, array.shape[2]), lambda i: (0, i, 0))

    whole = pl.BlockSpec((1, tile, WIDTH), lambda i: (0, i, 0))
    out = jax.ShapeDtypeStruct((1, ROWS, WIDTH), BF16)
    return pl.pallas_call(
        finish_kernel,
        grid=(steps,),
        out_shape=(out,) * 4,
        in_specs=[SCALARS] + [spec(array) for array in arrays],
        out_specs=(whole,) * 4,
        compiler_params=pltpu.CompilerParams(vmem_limit_bytes=VMEM_LIMIT),
        cost_estimate=NO_COST,
        name="finish",
    )(place, *arrays)


def body(q, k, v, tq, tk, tv, cot, out_weight):
    place = [lax.axis_index("c"), lax.axis_index("x") % 2, lax.axis_index("z")]
    place = jnp.stack(place).astype(jnp.int32)
    arrays = (q, tq, k, tk, v, tv)

    shard = lax.dynamic_slice_in_dim(out_weight, place[1] * HALF, HALF, axis=1)
    shard = permute(shard, swap_low_and_core)
    pair = lax.dynamic_slice_in_dim(cot[0], (1 - place[1]) * HALF, HALF, axis=1)
    pair = permute(pair, to_pair)
    pair_near = permute(pair, to_sibling)
    sib_kv, sib_q = pack_call(
        pack_first_kernel, "pack_first", [0] * 7, [8, 6], place, *arrays, cot
    )
    near = permute(sib_kv, to_sibling)
    near_q = permute(sib_q, to_sibling)
    (far,) = pack_call(
        pack_halo_kernel, "pack_halo", [0] * 4 + [8, None, None], [16],
        place, k, tk, v, tv, near, pair, shard,
    )
    pieces = ring(shard)
    far = permute(far, to_chip(1))

    grad, grad_pair = project(place, cot, near_q, pair, pair_near, pieces)
    grad_pair = permute(grad_pair, to_pair)

    tan = tangents(place, arrays, near, near_q, far, grad)
    tan_pair = permute(tan, to_pair)

    def chunk_grads(chunk, first):
        return gradients(place, chunk, q, k, v, near, near_q, far, grad, grad_pair, first)

    q0, own0, sib0, back0 = chunk_grads(0, tan)
    back0 = permute(back0, to_chip(-1))
    q1, own1, sib1, back1, cross1 = chunk_grads(1, q0)
    back1 = permute(back1, to_chip(-1))
    cross1 = permute(cross1, to_chip(-1, cross=True))
    tan_own, tan_pair, own_sib, pair_sib = tangent(place, tan, tan_pair, pieces, q1)
    added = add(tan_pair, permute(pair_sib, to_sibling))
    tan_pair = permute(added, to_pair)
    own0, sib = total(
        total_first_kernel, "total_first", [2, 8], COST,
        own0, sib0, sib1, own_sib, back0, first=(added,),
    )
    sib = permute(sib, to_sibling)
    own1, cross1 = total(
        total_last_kernel, "total_last", [2, 2], BIG_COST, own1, back1, cross1, first=()
    )
    return finish(place, q0, q1, own0, own1, sib, cross1, tan_own, tan_pair)


def solution(mesh):
    cut = Mesh(mesh.devices.reshape(SIZES), AXES)
    rows = P(("yl", "z"), ("x", "yh", "c"), None)
    return jax.shard_map(
        body,
        mesh=cut,
        in_specs=(rows,) * 7 + (P(("yl", "z"), None),),
        out_specs=(rows,) * 4,
        check_vma=False,
    )
```

```python
import jax
import jax.numpy as jnp
from jax import lax
from jax.experimental import pallas as pl
from jax.experimental.pallas import tpu as pltpu
from jax.sharding import Mesh
from jax.sharding import PartitionSpec as P

HEADS = 20
HEAD_DIM = 128
ROWS = 128
WIDTH = HEADS * HEAD_DIM
HALF = WIDTH // 2
PART = WIDTH // 4
PART_HEADS = HEADS // 4
FACTOR = HEAD_DIM ** (-0.5)

AXES = ("yl", "z", "x", "yh", "c")
SIZES = (2, 8, 4, 2, 2)

F32 = jnp.float32
BF16 = jnp.bfloat16
VMEM_LIMIT = 60 * 1024 * 1024
SMALL_LIMIT = 28 * 1024 * 1024
COST = pl.CostEstimate(flops=10**10, bytes_accessed=10**7, transcendentals=0)


def permute(block, move):
    route = []
    for index in range(256):
        rest, place = index, []
        for size in reversed(SIZES):
            place.append(rest % size)
            rest //= size
        goal = 0
        for coordinate, size in zip(move(*reversed(place)), SIZES):
            goal = goal * size + coordinate
        route.append((index, goal))
    return lax.ppermute(block, AXES, route)


def to_chip(step, cross=False):
    def move(yl, z, x, yh, c):
        chip = (x * 2 + yh + step) % 8
        return yl, z, chip // 2, chip % 2, (1 - c if cross else c)

    return move


def to_sibling(yl, z, x, yh, c):
    return yl, z, x, yh, 1 - c


def to_pair(yl, z, x, yh, c):
    return yl, z, x ^ 1, yh, c


def swap_low_and_core(yl, z, x, yh, c):
    return c, z, x, yh, yl


def columns(part, width=PART):
    return pl.ds(pl.multiple_of(part * width, width), width)


def dot(a, b, dims):
    return lax.dot_general(a, b, (dims, ((), ())), preferred_element_type=F32)


NT = ((1,), (1,))
NN = ((1,), (0,))
TN = ((0,), (0,))
ANYWHERE = pl.BlockSpec(memory_space=pl.ANY)
SCALARS = pl.BlockSpec(memory_space=pltpu.SMEM)


def stacked(n):
    return jax.ShapeDtypeStruct((n, ROWS, PART), BF16)


def pack_call(kernel, name, inputs, outputs, *arrays):
    steps = 2
    tile = ROWS // steps

    def spec(n):
        if n is None:
            return ANYWHERE
        if n == 0:
            return pl.BlockSpec((1, tile, WIDTH), lambda i: (0, i, 0))
        return pl.BlockSpec((n, tile, PART), lambda i: (0, i, 0))

    return pl.pallas_call(
        kernel,
        grid=(steps,),
        out_shape=[stacked(n) for n in outputs],
        in_specs=[SCALARS] + [spec(n) for n in inputs],
        out_specs=[spec(n) for n in outputs],
        compiler_params=pltpu.CompilerParams(vmem_limit_bytes=VMEM_LIMIT),
        cost_estimate=COST,
        name=name,
    )(*arrays)


def pack_first_kernel(place, q, tq, k, tk, v, tv, cot, own, sib, pair):
    core, side = place[0], place[1]
    for entry, source in enumerate((k, tk, v, tv, q, tq)):
        if entry < 4:
            own[entry] = source[0, :, columns(2 * core)]
        sib[entry] = source[0, :, columns(2 - 2 * core)]
    for entry, source in enumerate((q, tq)):
        sib[6 + entry] = source[0, :, columns(3 - 2 * core)]
    for entry in range(2):
        sib[8 + entry] = cot[0, :, columns(2 * side + entry)]
        pair[entry] = cot[0, :, columns(2 - 2 * side + entry)]


def pack_second_kernel(place, k, tk, v, tv, near, far, sib):
    core = place[0]
    for entry, source in enumerate((k, tk, v, tv)):
        far[entry] = near[entry]
        far[4 + entry] = source[0, :, columns(2 * core + 1)]
        sib[entry] = source[0, :, columns(3 - 2 * core)]


def pass_kernel(rows, first, out):
    del first
    out[...] = rows[...]


def after(rows, first):
    whole = pl.BlockSpec(memory_space=pltpu.VMEM)
    return pl.pallas_call(
        pass_kernel,
        out_shape=jax.ShapeDtypeStruct(rows.shape, BF16),
        in_specs=[whole, ANYWHERE],
        out_specs=whole,
        compiler_params=pltpu.CompilerParams(vmem_limit_bytes=SMALL_LIMIT),
        cost_estimate=pl.CostEstimate(flops=1, bytes_accessed=1, transcendentals=0),
        name="after",
    )(rows, first)


def project_kernel(place, cot, near, pair, pair_near, weight, first, own, send0, send1, rows):
    del place, first
    step = pl.program_id(0)

    @pl.when(step == 0)
    def _():
        rows[:ROWS, :] = cot[0]
        for block, ref in enumerate((near, pair, pair_near)):
            start = (block + 1) * ROWS
            rows[start : start + ROWS, :PART] = ref[0]
            rows[start : start + ROWS, PART:] = ref[1]

    out = dot(rows[...], weight[...], NT)
    own[...] = out[: 2 * ROWS]
    for chunk, send in enumerate((send0, send1)):

        @pl.when(step == chunk)
        def _(send=send):
            send[...] = out[2 * ROWS :].astype(BF16)


def project(place, cot, near, pair, pair_near, weight, first):
    def stack(start):
        return pl.BlockSpec((2, ROWS, PART), lambda i, place: (start, 0, 0))

    block = pl.BlockSpec((2 * ROWS, PART), lambda i, place: (0, 0))
    send = jax.ShapeDtypeStruct((2 * ROWS, PART), BF16)
    return pl.pallas_call(
        project_kernel,
        out_shape=(jax.ShapeDtypeStruct((2 * ROWS, HALF), F32), send, send),
        grid_spec=pltpu.PrefetchScalarGridSpec(
            num_scalar_prefetch=1,
            grid=(2,),
            in_specs=[
                pl.BlockSpec((1, ROWS, HALF), lambda i, place: (0, 0, place[1])),
                stack(4),
                stack(0),
                stack(0),
                pl.BlockSpec((PART, HALF), lambda i, place: (i, 0)),
                ANYWHERE,
            ],
            out_specs=(
                pl.BlockSpec((2 * ROWS, PART), lambda i, place: (0, i)), block, block
            ),
            scratch_shapes=[pltpu.VMEM((4 * ROWS, HALF), BF16)],
        ),
        compiler_params=pltpu.CompilerParams(vmem_limit_bytes=SMALL_LIMIT),
        cost_estimate=COST,
        name="project",
    )(place, cot, near, pair, pair_near, weight, first)


def attend_head(core, chunk, head, refs):
    q, tq, k, tk, v, tv, near, near_q, far_own, far_sib, grad_own, grad_pair, *outs = refs
    own_q, own_kv, sib_out, back_own, back_sib, tan_out = outs
    start = head * HEAD_DIM
    cols = slice(start, start + HEAD_DIM)
    start += chunk * PART
    grad_cols = slice(start, start + HEAD_DIM)
    start += core * HALF
    raw = slice(start, start + HEAD_DIM)
    far_entry = 4 * chunk
    sib_far = 4 if chunk == 0 else 4

    def ordered(own, sib):
        return [own, sib] if core == 0 else [sib, own]

    def window(entry, source):
        blocks = ordered(far_own[far_entry + entry, :, cols], far_sib[entry, :, cols]) + ordered(
            source[0, :, raw], near[entry, :, cols]
        )
        return jnp.concatenate(blocks, axis=0)

    key, tkey, value, tvalue = (window(i, source) for i, source in enumerate((k, tk, v, tv)))
    query = ordered(q[0, :, raw], near_q[4 + 2 * chunk, :, cols])
    tquery = ordered(tq[0, :, raw], near_q[5 + 2 * chunk, :, cols])
    grad = (grad_own[:, grad_cols] + grad_pair[:, cols].astype(F32)).astype(BF16)
    grad = ordered(grad[:ROWS], grad[ROWS:])
    both_key = jnp.concatenate([key, tkey], axis=1)
    span = 3 * ROWS
    zero = jnp.zeros((ROWS, ROWS), BF16)
    probs, gss, tans, qgs = [], [], [], []
    for block in range(2):
        seen = slice(block * ROWS, block * ROWS + span)
        scores = dot(query[block], key[seen], NT)
        both_query = jnp.concatenate([tquery[block], query[block]], axis=1)
        tan_scores = dot(both_query, both_key[seen], NT)
        grad_prob = dot(grad[block], value[seen], NT)
        top = jnp.max(scores, axis=-1, keepdims=True)
        expos = jnp.exp((scores - top) * FACTOR)
        prob = expos * (1.0 / jnp.sum(expos, axis=-1, keepdims=True))
        prob_b = prob.astype(BF16)
        mean = jnp.sum(prob * tan_scores, axis=-1, keepdims=True)
        scaled = prob * FACTOR
        tan_prob = (scaled * (tan_scores - mean)).astype(BF16)
        delta = jnp.sum(prob_b.astype(F32) * grad_prob, axis=-1, keepdims=True)
        gs = (scaled * (grad_prob - delta)).astype(BF16)
        tans.append(dot(prob_b, tvalue[seen], NN) + dot(tan_prob, value[seen], NN))
        qgs.append(dot(gs, key[seen], NN))
        fill = [prob_b, zero] if block == 0 else [zero, prob_b]
        probs.append(jnp.concatenate(fill, axis=1))
        fill = [gs, zero] if block == 0 else [zero, gs]
        gss.append(jnp.concatenate(fill, axis=1))
    kg = dot(jnp.concatenate(gss, axis=0), jnp.concatenate(query, axis=0), TN)
    vg = dot(jnp.concatenate(probs, axis=0), jnp.concatenate(grad, axis=0), TN)

    def block_of(whole, index):
        return whole[index * ROWS : (index + 1) * ROWS]

    tan_out[:ROWS, cols] = tans[core].astype(BF16)
    tan_out[ROWS:, cols] = tans[1 - core].astype(BF16)
    own_q[0, :, cols] = qgs[core].astype(BF16)
    sib_out[0, :, cols] = qgs[1 - core].astype(BF16)
    for entry, terms in enumerate((kg, vg)):
        back_own[entry, :, cols] = block_of(terms, core).astype(BF16)
        back_sib[entry, :, cols] = block_of(terms, 1 - core).astype(BF16)
        own_kv[entry, :, cols] = block_of(terms, 2 + core)
        sib_out[1 + entry, :, cols] = block_of(terms, 3 - core).astype(BF16)


def attend(place, chunk, *arrays):
    def kernel(place, *refs):
        for core in range(2):

            @pl.when(place[0] == core)
            def _(core=core):
                for head in range(PART_HEADS):
                    attend_head(core, chunk, head, refs)

    whole = pl.BlockSpec(memory_space=pltpu.VMEM)

    def out(n, dtype):
        return jax.ShapeDtypeStruct((n, ROWS, PART), dtype)

    return pl.pallas_call(
        kernel,
        out_shape=(
            out(1, BF16), out(2, F32), out(3, BF16), out(2, BF16), out(2, BF16),
            jax.ShapeDtypeStruct((2 * ROWS, PART), BF16),
        ),
        in_specs=[SCALARS] + [whole] * len(arrays),
        out_specs=(whole,) * 6,
        compiler_params=pltpu.CompilerParams(vmem_limit_bytes=SMALL_LIMIT),
        cost_estimate=COST,
        name="attend",
    )(place, *arrays)


def tangent_kernel(place, tan0, tan1, weight0, weight1, back, cross, near, own, sib, total):
    del place, back, cross, near
    step = pl.program_id(0)
    for half, weight in enumerate((weight0, weight1)):

        @pl.when(step == 2 * half)
        def _(weight=weight):
            total[...] = dot(tan0[...], weight[...], NN)

        @pl.when(step == 2 * half + 1)
        def _(weight=weight):
            both = total[...] + dot(tan1[...], weight[...], NN)
            own[0] = both[:ROWS]
            sib[0] = both[ROWS:].astype(BF16)


def tangent(place, tan0, tan1, weight0, weight1, *earlier):
    whole = pl.BlockSpec((2 * ROWS, PART), lambda i, place: (0, 0))
    block = pl.BlockSpec((1, ROWS, HALF), lambda i, place: (i // 2, 0, 0))
    return pl.pallas_call(
        tangent_kernel,
        out_shape=(
            jax.ShapeDtypeStruct((2, ROWS, HALF), F32),
            jax.ShapeDtypeStruct((2, ROWS, HALF), BF16),
        ),
        grid_spec=pltpu.PrefetchScalarGridSpec(
            num_scalar_prefetch=1,
            grid=(4,),
            in_specs=[
                whole,
                whole,
                pl.BlockSpec((PART, HALF), lambda i, place: (jnp.minimum(i, 1), 0)),
                pl.BlockSpec((PART, HALF), lambda i, place: (jnp.maximum(i, 2) - 2, 0)),
            ]
            + [ANYWHERE] * len(earlier),
            out_specs=(block, block),
            scratch_shapes=[pltpu.VMEM((2 * ROWS, HALF), F32)],
        ),
        compiler_params=pltpu.CompilerParams(vmem_limit_bytes=SMALL_LIMIT),
        cost_estimate=COST,
        name="tangent",
    )(place, tan0, tan1, weight0, weight1, *earlier)


def finish_first_kernel(place, own0, own1, sib0, sib1, tan_own, tan_sib, q_out, tan_out):
    core, side = place[0], place[1]
    for chunk, (own, sib) in enumerate(((own0, sib0), (own1, sib1))):
        q_out[0, :, columns(2 * core + chunk)] = own[0]
        q_out[0, :, columns(2 - 2 * core + chunk)] = sib[0]
    for entry, half in enumerate((side, 1 - side)):
        tan_out[0, :, columns(half, HALF)] = (
            tan_own[entry] + tan_sib[entry].astype(F32)
        ).astype(BF16)


def finish_last_kernel(
    place, own0, own1, sib0, sib1, near0, near1, cross0, cross1, k_out, v_out
):
    core = place[0]
    chunks = ((own0, sib0, near0, cross0), (own1, sib1, near1, cross1))
    for chunk, (own, sib, near, cross) in enumerate(chunks):
        for entry, ref in enumerate((k_out, v_out)):
            ref[0, :, columns(2 * core + chunk)] = (
                own[entry] + near[entry].astype(F32)
            ).astype(BF16)
            ref[0, :, columns(2 - 2 * core + chunk)] = (
                sib[entry + 1].astype(F32) + cross[entry].astype(F32)
            ).astype(BF16)


def finish(kernel, name, place, *arrays):
    whole = pl.BlockSpec(memory_space=pltpu.VMEM)
    out = jax.ShapeDtypeStruct((1, ROWS, WIDTH), BF16)
    return pl.pallas_call(
        kernel,
        out_shape=(out, out),
        in_specs=[SCALARS] + [whole] * len(arrays),
        out_specs=(whole, whole),
        compiler_params=pltpu.CompilerParams(vmem_limit_bytes=SMALL_LIMIT),
        cost_estimate=COST,
        name=name,
    )(place, *arrays)


def body(q, k, v, tq, tk, tv, cot, out_weight):
    place = jnp.stack([lax.axis_index("c"), lax.axis_index("x") % 2]).astype(jnp.int32)
    arrays = (q, tq, k, tk, v, tv)

    def gathered(shard):
        return lax.all_gather(shard, "z", axis=0, tiled=True)

    def swapped(half):
        shard = lax.dynamic_slice_in_dim(out_weight, half * HALF, HALF, axis=1)
        return permute(shard, swap_low_and_core)

    shard_a, shard_b = swapped(place[1]), swapped(1 - place[1])
    weight_a = gathered(shard_a)
    own, sib, pair = pack_call(
        pack_first_kernel, "pack_first", [0] * 7, [4, 10, 2], place, *arrays, cot
    )
    near_0 = permute(sib, to_sibling)
    far_a = permute(own, to_chip(1))
    pair = permute(pair, to_pair)
    far, sib = pack_call(
        pack_second_kernel, "pack_second", [0] * 4 + [10], [8, 4], place, k, tk, v, tv, near_0
    )
    near_1 = permute(sib, to_sibling)
    far_b = permute(far, to_chip(1))
    far_c = permute(near_1, to_chip(1))
    pair_near = permute(after(pair, far), to_sibling)

    grad, send_0, send_1 = project(place, cot, near_0, pair, pair_near, weight_a, far)
    weight_b = gathered(shard_b)
    grad_0 = permute(send_0, to_pair)
    grad_1 = permute(send_1, to_pair)

    def chunk_grads(chunk, *others):
        own_q, own_kv, sib, back_own, back_sib, tan = attend(place, chunk, *arrays, *others)
        back_own = permute(back_own, to_chip(-1))
        back_sib = permute(back_sib, to_chip(-1, cross=True))
        return own_q, own_kv, permute(sib, to_sibling), back_own, back_sib, tan

    q0, kv0, sib0, back0, cross0, tan0 = chunk_grads(
        0, near_0, near_0, far_a, far_b, grad, grad_0
    )
    q1, kv1, sib1, back1, cross1, tan1 = chunk_grads(
        1, near_1, near_0, far_b, far_c, grad, grad_1
    )
    tan_own, tan_sib = tangent(
        place, tan0, tan1, weight_a, weight_b, back0, cross0, sib0
    )
    tan_sib = permute(tan_sib, to_sibling)
    query_grad, tangent_out = finish(
        finish_first_kernel, "finish_first", place, q0, q1, sib0, sib1, tan_own, tan_sib
    )
    key_grad, value_grad = finish(
        finish_last_kernel, "finish_last", place,
        kv0, kv1, sib0, sib1, back0, back1, cross0, cross1,
    )
    return tangent_out, query_grad, key_grad, value_grad


def solution(mesh):
    cut = Mesh(mesh.devices.reshape(SIZES), AXES)
    rows = P(("yl", "z"), ("x", "yh", "c"), None)
    return jax.shard_map(
        body,
        mesh=cut,
        in_specs=(rows,) * 7 + (P(("yl", "z"), None),),
        out_specs=(rows,) * 4,
        check_vma=False,
    )
```
